32 devices in a mesh: var: 8 (over y, x, core), tp: 4 (over z).
Axes of the slice: x: 2, y: 2, z: 4, core: 2. Of those that a mesh axis runs over, the one named last changes fastest.
Arguments:
- projected: bfloat16 [64, 32, 3, 8192], P(('var', 'tp')), may hold values from -6 to 6
- cache_history: bfloat16 [48, 127, 8192], P('var', None, 'tp'), may hold values from -6 to 6
- cache_inputs: bfloat16 [48, 6, 3, 8192], P('var', None, None, 'tp'), may hold values from -6 to 6
- feature_taps: bfloat16 [7, 3, 8192], P(None, None, 'tp'), may hold values from -2 to 2
- filters: bfloat16 [128, 512], P(None, 'tp'), may hold values from -0.5 to 0.5
- skip_weight: bfloat16 [8192], P('tp'), may hold values from -4 to 4
- base_inputs: bfloat16 [4, 3, 8192], P(None, None, 'tp'), may hold values from -6 to 6
- window_owner: int32 [64, 1], replicated, may hold values from 0 to 7; in each aligned block of 8 rows (0 to 7, 8 to 15, ...) at most 2 rows name the same one
- window_slot: int32 [64], replicated, may hold values from 0 to 5
- variant_position: int32 [64], P('var'), may hold values from 0 to 31
- allele: int32 [64], P('var'), may hold values from 0 to 3
Outputs:
- mixer_out: bfloat16 [64, 32, 8192], P(('var', 'tp'))
The draws below stay inside these ranges and needn't reach their ends.
Inputs may be any that keep to these rules, and one draw needn't show every extreme that they name: `window_owner`: among the windows of one index of var (aligned blocks of 8 rows), at most 2 name the same owner.
All inputs are finite; a program needn't handle non-finite values.
Results may differ from the reference program's by a relative error of at most 0.0049.
Values may be sent and summed in bfloat16 or wider, within the bound.
A program may use at most 128 MiB of HBM per device.

```python
import math
import jax
import jax.numpy as jnp
import numpy as np
from jax import lax

D = 8192
FGROUP = 16
FEAT_TAPS = 7
FILT_TAPS = 128
BASES = 4
WLEN = 32
SLOTS = 6
WIN_DEV = 8
CAP = 2
WINDOWS = 64
LOCI = 48
OWNERS = 8
N_VAR = 8


def with_ends(entries, key, low, high):
    place = [jax.random.randint(jax.random.fold_in(key, axis), (), 0, length) for axis, length in enumerate(entries.shape)]
    widest = entries.shape.index(max(entries.shape))
    beside = place[:widest] + [(place[widest] + 1) % entries.shape[widest]] + place[widest + 1:]
    return entries.at[tuple(place)].set(low).at[tuple(beside)].set(high)


def levels(key, dims, cuts, least, top_value):
    def one(dim, shards_of):
        draws = jax.random.uniform(jax.random.fold_in(jax.random.fold_in(key, 6), dim), (shards_of,), jnp.float32, least / len(cuts), top_value / len(cuts))
        return jnp.repeat(jnp.exp(draws), dims[dim] // shards_of).reshape((-1,) + (1,) * (len(dims) - dim - 1))

    gain = one(*cuts[0])
    for cut in cuts[1:]:
        gain = gain * one(*cut)
    return gain


def deal_out(own_key, own, number, rows, number_of, top, bound, skew):
    sequence = jax.random.permutation(own_key, number_of)
    packed, common = shares(number_of, rows * top, bound, skew, True), shares(number_of, rows * top, bound, skew, False)
    places = jnp.arange(number_of)

    def named(lengths, offset_by):
        used = int((lengths > 0).sum())
        fixed = max(1, used // 4)
        passed = fixed + (places - fixed + offset_by * (used - fixed)) % max(1, number_of - fixed)
        return jnp.zeros((number_of,), jnp.int32).at[sequence[jnp.where(places < fixed, places, passed)]].set(jnp.asarray(lengths, jnp.int32))

    lengths = jnp.where(number % 4 == 0, named(packed, number // 4), named(common, number - number // 4 - 1))
    mixed = jax.random.permutation(jax.random.fold_in(own, 3), number_of)
    donor, taker = mixed[0:number_of // 2 * 2:2], mixed[1:number_of // 2 * 2:2]
    room = jnp.minimum(lengths[donor] - 1, bound - lengths[taker]) // 2
    room = jnp.where((donor == sequence[0]) | (taker == sequence[0]) | (lengths[taker] == 0), 0, jnp.maximum(room, 0))
    passed = jax.random.randint(jax.random.fold_in(own, 4), (number_of // 2,), 0, 1 << 20) % (room + 1)
    lengths = lengths.at[donor].add(-passed).at[taker].add(passed)
    members = jnp.searchsorted(jnp.cumsum(lengths), jnp.arange(rows * top), side="right").astype(jnp.int32)
    listing = members.reshape(top, rows).T
    listing = listing[jax.random.permutation(jax.random.fold_in(own, 1), rows)]
    offset_by = jax.random.randint(jax.random.fold_in(own, 2), (rows, 1), 0, top)
    return jnp.take_along_axis(listing, (jnp.arange(top)[None, :] + offset_by) % top, axis=1)


def shares(number_of, total, reach, skew, full):
    loads = [(1 << 20) // math.isqrt(rank ** skew) + 1 for rank in range(1, number_of + 1)]
    largest = reach if full else min(reach, max(-(-total // number_of), total * loads[0] // sum(loads)))
    least = 1 if total - largest >= number_of - 1 else 0
    counts, surplus = [largest] + [least] * (number_of - 1), total - largest - least * (number_of - 1)
    while surplus > 0:
        free = [i for i in range(1, number_of) if counts[i] < largest] or [i for i in range(1, number_of) if counts[i] < reach]
        whole, left = sum([loads[i] for i in free]), surplus
        for i in free:
            extra = min(reach - counts[i], max(1, left * loads[i] // whole), surplus)
            counts[i] = counts[i] + extra
            surplus = surplus - extra
    return np.array(counts)


def scatter_about(rng, extent, spread, limit, split=(), dtype=jnp.bfloat16):
    array = spread * jax.random.normal(rng, extent, jnp.float32)
    if split:
        array = array * levels(rng, extent, split, -0.22, 0.18)
    return jnp.clip(array, -limit, limit).astype(dtype)


def setup_inputs(seed: int = 0) -> dict:
    key_of = jax.random.split(jax.random.key(seed), 12)
    projected = scatter_about(key_of[0], (WINDOWS, WLEN, 3, D), 1.0, 6.0, ((0, 32),))
    cache_history = scatter_about(key_of[1], (LOCI, FILT_TAPS - 1, D), 1.0, 6.0, ((0, 8), (2, 4)))
    cache_inputs = scatter_about(key_of[2], (LOCI, FEAT_TAPS - 1, 3, D), 1.0, 6.0, ((0, 8), (3, 4)))
    feature_taps = scatter_about(key_of[3], (FEAT_TAPS, 3, D), FEAT_TAPS ** -0.5, 2.0, ((2, 4),))
    filters = scatter_about(key_of[4], (FILT_TAPS, D // FGROUP), FILT_TAPS ** -0.5, 0.5, ((1, 4),))
    skip_weight = scatter_about(key_of[5], (D,), 1.0, 4.0, ((0, 4),))
    base_inputs = scatter_about(key_of[6], (BASES, 3, D), 1.0, 6.0, ((2, 4),))
    window_owner_keys = jax.random.split(jax.random.fold_in(key_of[7], 1), WINDOWS // WIN_DEV)
    window_owner_turns = jax.random.permutation(jax.random.fold_in(key_of[7], 3), WINDOWS // WIN_DEV)
    window_owner = jax.vmap(lambda own, number: deal_out(jax.random.fold_in(key_of[7], 2), own, number, WIN_DEV, OWNERS, 1, CAP, 2))(window_owner_keys, window_owner_turns).reshape((WINDOWS, 1))
    window_slot = with_ends(jax.random.randint(key_of[8], (WINDOWS,), 0, SLOTS), jax.random.fold_in(key_of[8], 1), 0, SLOTS - 1).astype(jnp.int32)
    variant_position = with_ends(jax.random.randint(key_of[9], (WINDOWS,), 0, WLEN), jax.random.fold_in(key_of[9], 1), 0, WLEN - 1).astype(jnp.int32)
    allele = with_ends(jax.random.randint(key_of[10], (WINDOWS,), 0, BASES), jax.random.fold_in(key_of[10], 1), 0, BASES - 1).astype(jnp.int32)
    return dict(projected=projected, cache_history=cache_history, cache_inputs=cache_inputs, feature_taps=feature_taps, filters=filters, skip_weight=skip_weight, base_inputs=base_inputs, window_owner=window_owner, window_slot=window_slot, variant_position=variant_position, allele=allele)


def tap_table(filters, row_count, col_count, offset):
    tap_count = filters.shape[0]
    lag_index = jnp.arange(row_count)[:, None] + offset - jnp.arange(col_count)[None, :]
    inside_range = (lag_index >= 0) & (lag_index < tap_count)
    picked = jnp.take(filters.astype(jnp.float32), jnp.clip(lag_index, 0, tap_count - 1), axis=0)
    return jnp.where(inside_range[:, :, None], picked, jnp.float32(0.0))


def grouped_filter(table, values):
    item_count, length, channel_count = values.shape
    groups = table.shape[2]
    shaped = values.reshape(item_count, length, groups, channel_count // groups)
    result = jnp.einsum("tsg,nsgc->ntgc", table, shaped)
    return result.reshape(item_count, table.shape[0], channel_count)


def reference(projected, cache_history, cache_inputs, feature_taps, filters, skip_weight, base_inputs, window_owner, window_slot, variant_position, allele):
    window_count = projected.shape[0]
    window_len = projected.shape[1]
    history_len = cache_history.shape[1]
    lead_len = cache_inputs.shape[1]
    locus = (window_owner[:, 0] * SLOTS + window_slot).astype(jnp.int32)
    table_win = tap_table(filters, window_len, window_len, 0)
    table_pre = tap_table(filters, window_len, history_len, history_len)

    def one_block(pieces):
        input_block, locus_block, position_block, allele_block = pieces
        base_rows = jnp.take(base_inputs, allele_block, axis=0)
        placed = jnp.arange(window_len)[None, :] == position_block[:, None]
        altered = jnp.where(placed[:, :, None, None], base_rows[:, None], input_block)
        extended = jnp.concatenate([jnp.take(cache_inputs, locus_block, axis=0), altered], axis=1)
        featured = jnp.zeros(altered.shape, jnp.float32)
        for tap_index in range(FEAT_TAPS):
            start_row = lead_len - tap_index
            featured = featured + feature_taps[tap_index].astype(jnp.float32) * extended[:, start_row:start_row + window_len].astype(jnp.float32)
        mixed_in = lax.optimization_barrier((featured[:, :, 1] * featured[:, :, 2]).astype(jnp.bfloat16)).astype(jnp.float32)
        inside = grouped_filter(table_win, mixed_in)
        history = jnp.take(cache_history, locus_block, axis=0).astype(jnp.float32)
        carried = lax.optimization_barrier(grouped_filter(table_pre, history).astype(jnp.bfloat16)).astype(jnp.float32)
        filtered = inside + carried + skip_weight.astype(jnp.float32) * mixed_in
        return (featured[:, :, 0] * filtered).astype(jnp.bfloat16)

    pieces = (projected.reshape((N_VAR, WIN_DEV) + projected.shape[1:]), locus.reshape(N_VAR, WIN_DEV), variant_position.reshape(N_VAR, WIN_DEV), allele.reshape(N_VAR, WIN_DEV))
    mixed_all = lax.map(one_block, pieces)
    return mixed_all.reshape(window_count, window_len, projected.shape[3])
```

```python
import functools

import jax
import jax.numpy as jnp
from jax import lax
from jax.experimental import pallas as pl
from jax.experimental.pallas import tpu as pltpu
from jax.sharding import PartitionSpec as P

LANES = 128
ROWS = 112
F32 = jnp.float32
BF16 = jnp.bfloat16


def skewed(rows, first, keep):
    parts = []
    for g in range(8):
        wide = jnp.broadcast_to(rows[g : g + 1], (32, LANES))
        wide = pltpu.roll(wide, first, 1, stride=1, stride_axis=0)
        parts.append(jnp.where(keep, wide, 0.0))
    return jnp.concatenate(parts, axis=0).astype(BF16)


def own_group(stacked, lane_group):
    out = stacked[0:32]
    for g in range(1, 8):
        out = jnp.where(lane_group == g, stacked[g * 32 : g * 32 + 32], out)
    return out


def kernel(
    n_var, n_tp, chunks, width,
    owner, slot, pos, allele, hist, lead, proj_far, taps, frev, base,
    out,
    owned, proj, all_taps, all_frev, ext, pick, rank,
    s1, r1, l1, s2, r2, l2, sp, rp, lp, lj,
    *blocks,
):
    send1, recv1, send2, recv2 = (blocks[k * chunks : (k + 1) * chunks] for k in range(4))
    slots = hist.shape[0]
    history = hist.shape[1]
    chan = hist.shape[2]
    local = pos.shape[0]
    group = chan // frev.shape[0]
    me = lax.axis_index("var")
    mt = lax.axis_index("tp")

    load_proj = pltpu.make_async_copy(proj_far, proj, lj.at[0])
    load_proj.start()
    barrier = pltpu.get_barrier_semaphore()

    def greet_var(d, _):
        pl.semaphore_signal(barrier, inc=1, device_id={"var": lax.rem(me + d, n_var)}, device_id_type=pl.DeviceIdType.MESH)
        return 0

    def greet_tp(d, _):
        pl.semaphore_signal(barrier, inc=1, device_id={"tp": lax.rem(mt + d, n_tp)}, device_id_type=pl.DeviceIdType.MESH)
        return 0

    lax.fori_loop(1, n_var, greet_var, 0)
    lax.fori_loop(1, n_tp, greet_tp, 0)
    pl.semaphore_wait(barrier, n_var - 1 + n_tp - 1)

    def param_copy(k, d, src, dst, landed, to):
        return pltpu.make_async_remote_copy(
            src_ref=src, dst_ref=dst.at[landed], send_sem=sp.at[k, d], recv_sem=rp.at[k, d],
            device_id={"tp": to}, device_id_type=pl.DeviceIdType.MESH)

    def hop1(q, d, row, landed, to):
        return pltpu.make_async_remote_copy(
            src_ref=send1[q].at[row], dst_ref=recv1[q].at[landed], send_sem=s1.at[q, d], recv_sem=r1.at[q, d],
            device_id={"var": to}, device_id_type=pl.DeviceIdType.MESH)

    def hop2(q, d, row, landed, to):
        return pltpu.make_async_remote_copy(
            src_ref=send2[q].at[row], dst_ref=recv2[q].at[landed], send_sem=s2.at[q, d], recv_sem=r2.at[q, d],
            device_id={"tp": to}, device_id_type=pl.DeviceIdType.MESH)

    def start_params(d, _):
        to = lax.rem(mt + d, n_tp)
        param_copy(0, d, taps, all_taps, mt, to).start()
        param_copy(1, d, frev, all_frev, mt, to).start()
        return 0

    lax.fori_loop(1, n_tp, start_params, 0)
    keep_taps = pltpu.make_async_copy(taps, all_taps.at[mt], lp.at[0])
    keep_frev = pltpu.make_async_copy(frev, all_frev.at[mt], lp.at[1])
    keep_taps.start()
    keep_frev.start()

    def picks(v, _):
        def one(i, state):
            count, first, second = state
            hit = (owner[v * local + i] == me).astype(jnp.int32)
            which = slot[v * local + i]
            first = first + jnp.where(count == 0, hit * which, 0)
            second = second + jnp.where(count == 1, hit * which, 0)
            return count + hit, first, second

        zero = jnp.int32(0)
        _, first, second = lax.fori_loop(0, local, one, (zero, zero, zero))
        pick[2 * v] = first
        pick[2 * v + 1] = second
        return 0

    lax.fori_loop(0, n_var, picks, 0)

    def ranks(w, _):
        def one(i, count):
            same = (owner[me * local + i] == owner[me * local + w]).astype(jnp.int32)
            return count + jnp.where(i < w, same, 0)

        rank[w] = lax.fori_loop(0, local, one, jnp.int32(0))
        return 0

    lax.fori_loop(0, local, ranks, 0)

    row32 = lax.broadcasted_iota(jnp.int32, (32, LANES), 0)
    lane32 = lax.broadcasted_iota(jnp.int32, (32, LANES), 1)
    lane_group = lane32 // group
    upper = lane32 >= row32
    lower = lane32 <= row32
    row16 = lax.broadcasted_iota(jnp.int32, (16, width), 0)
    row8 = lax.broadcasted_iota(jnp.int32, (8, width), 0)
    pairs = width // (2 * LANES)

    def carry_chunk(q):
        def body(b, _):
            at = b * (2 * LANES)
            lanes0 = q * width + at
            rows = frev[pl.ds(pl.multiple_of(lanes0 // group, 16), 16), :].astype(F32)
            for half in range(2):
                table = skewed(rows[half * 8 : half * 8 + 8], 0, upper)[:, :history]
                here = pl.ds(pl.multiple_of(lanes0 + half * LANES, LANES), LANES)
                there = pl.ds(pl.multiple_of(at + half * LANES, LANES), LANES)
                for n in range(slots):
                    got = jnp.dot(table, hist[n, :, here], preferred_element_type=F32)
                    owned[n, :, there] = own_group(got, lane_group).astype(BF16)
            return 0

        lax.fori_loop(0, pairs, body, 0)
        chunk = pl.ds(q * width, width)

        def fill(v, _):
            a, b = pick[2 * v], pick[2 * v + 1]
            send1[q][v, 0:32, :] = owned[a]
            send1[q][v, 32:64, :] = owned[b]
            for s in range(3):
                both = jnp.where(row16 < 8, lead[a, s, :, chunk].astype(F32), lead[b, s, :, chunk].astype(F32))
                send1[q][v, 64 + 16 * s : 80 + 16 * s, :] = both.astype(BF16)
            return 0

        lax.fori_loop(0, n_var, fill, 0)

        def start(d, _):
            to = lax.rem(me + d, n_var)
            hop1(q, d, to, me, to).start()
            return 0

        lax.fori_loop(1, n_var, start, 0)
        pltpu.make_async_copy(send1[q].at[me], recv1[q].at[me], l1.at[q]).start()

    for q in range(chunks):
        carry_chunk(q)

    def finish_params(d, _):
        src = lax.rem(mt + n_tp - d, n_tp)
        to = lax.rem(mt + d, n_tp)
        param_copy(0, d, taps, all_taps, src, to).wait_recv()
        param_copy(1, d, frev, all_frev, src, to).wait_recv()
        param_copy(0, d, taps, all_taps, mt, to).wait_send()
        param_copy(1, d, frev, all_frev, mt, to).wait_send()
        return 0

    lax.fori_loop(1, n_tp, finish_params, 0)
    keep_taps.wait()
    keep_frev.wait()

    def route(q):
        def arrive(d, _):
            hop1(q, d, lax.rem(me + d, n_var), lax.rem(me + n_var - d, n_var), lax.rem(me + d, n_var)).wait_recv()
            return 0

        lax.fori_loop(1, n_var, arrive, 0)
        pltpu.make_async_copy(send1[q].at[me], recv1[q].at[me], l1.at[q]).wait()
        chunk = pl.ds(q * width, width)

        def fill(t, _):
            for i in range(2):
                w = 2 * t + i
                o, r = owner[me * local + w], rank[w]
                send2[q][t, 32 * i : 32 * i + 32, :] = jnp.where(
                    r == 0, recv1[q][o, 0:32, :].astype(F32), recv1[q][o, 32:64, :].astype(F32)
                ).astype(BF16)
            for s in range(3):
                halves = []
                for i in range(2):
                    w = 2 * t + i
                    o, r = owner[me * local + w], rank[w]
                    both = recv1[q][o, 64 + 16 * s : 80 + 16 * s, :].astype(F32)
                    half = jnp.where(r == 0, both[0:8], both[8:16])
                    token = base[allele[w], :, chunk]
                    halves.append(jnp.where(row8 == 0, token[s : s + 1], half))
                send2[q][t, 64 + 16 * s : 80 + 16 * s, :] = jnp.concatenate(halves, axis=0).astype(BF16)
            return 0

        lax.fori_loop(0, n_tp, fill, 0)

        def start(d, _):
            to = lax.rem(mt + d, n_tp)
            hop2(q, d, to, mt, to).start()
            return 0

        lax.fori_loop(1, n_tp, start, 0)
        pltpu.make_async_copy(send2[q].at[mt], recv2[q].at[mt], l2.at[q]).start()

    def mix(q):
        def arrive(d, _):
            hop2(q, d, lax.rem(mt + d, n_tp), lax.rem(mt + n_tp - d, n_tp), lax.rem(mt + d, n_tp)).wait_recv()
            return 0

        lax.fori_loop(1, n_tp, arrive, 0)
        pltpu.make_async_copy(send2[q].at[mt], recv2[q].at[mt], l2.at[q]).wait()

        def body(step, _):
            c = step // pairs
            at = (step % pairs) * (2 * LANES)
            lanes0 = q * width + at
            rows = all_frev[c, pl.ds(pl.multiple_of(lanes0 // group, 16), 16), :].astype(F32)
            for half in range(2):
                table = skewed(rows[half * 8 : half * 8 + 8], 1, lower)[:, :32]
                here = pl.ds(pl.multiple_of(lanes0 + half * LANES, LANES), LANES)
                there = pl.ds(pl.multiple_of(at + half * LANES, LANES), LANES)
                glob = pl.ds(pl.multiple_of(c * chan + lanes0 + half * LANES, LANES), LANES)
                par = all_taps[c, :, here].astype(F32)
                gates, mixes = [], []
                for w in range(2):
                    place = row32 == pos[2 * mt + w]
                    feats = []
                    for s in range(3):
                        k = (half * 2 + w) * 3 + s
                        before = recv2[q][c, 64 + 16 * s : 80 + 16 * s, there].astype(F32)[8 * w : 8 * w + 8]
                        altered = jnp.where(place, before[0:1], proj[w, s, :, glob].astype(F32))
                        ext[k, 0:8, :] = before
                        ext[k, 8:40, :] = altered
                        total = par[8 * s : 8 * s + 1] * altered
                        for j in range(1, 7):
                            total = total + par[8 * s + j : 8 * s + j + 1] * ext[k, 8 - j : 40 - j, :]
                        feats.append(total)
                    gates.append(feats[0])
                    mixes.append((feats[1] * feats[2]).astype(BF16))
                got = jnp.dot(table, jnp.concatenate(mixes, axis=1), preferred_element_type=F32)
                for w in range(2):
                    inside = own_group(got[:, w * LANES : (w + 1) * LANES], lane_group)
                    carried = recv2[q][c, 32 * w : 32 * w + 32, there].astype(F32)
                    filtered = inside + carried + par[24:25] * mixes[w].astype(F32)
                    out[w, :, glob] = (gates[w] * filtered).astype(BF16)
            return 0

        lax.fori_loop(0, n_tp * pairs, body, 0)

    load_proj.wait()
    for q in range(min(2, chunks)):
        route(q)
    for q in range(chunks):
        mix(q)
        if q + 2 < chunks:
            route(q + 2)

    for q in range(chunks):
        def one(d, _, q=q):
            to = lax.rem(me + d, n_var)
            hop1(q, d, to, me, to).wait_send()
            return 0

        def two(d, _, q=q):
            to = lax.rem(mt + d, n_tp)
            hop2(q, d, to, mt, to).wait_send()
            return 0

        lax.fori_loop(1, n_var, one, 0)
        lax.fori_loop(1, n_tp, two, 0)


def local(projected, cache_history, cache_inputs, feature_taps, filters, skip_weight, base_inputs,
          window_owner, window_slot, variant_position, allele):
    n_var, n_tp = lax.axis_size("var"), lax.axis_size("tp")
    slots, history, chan = cache_history.shape
    window_len, full = projected.shape[1], projected.shape[3]
    width = min(512, chan)
    chunks = chan // width
    proj = projected.transpose(0, 2, 1, 3)
    lead = jnp.pad(cache_inputs.transpose(0, 2, 1, 3), ((0, 0), (0, 0), (2, 0), (0, 0)))
    lead = jnp.concatenate([lead, lead], axis=2)
    taps = jnp.pad(feature_taps.transpose(1, 0, 2), ((0, 0), (0, 1), (0, 0))).reshape(24, chan)
    taps = jnp.concatenate([taps, jnp.pad(skip_weight[None], ((0, 7), (0, 0)))], axis=0)
    frev = filters[::-1].T
    base = jnp.pad(base_inputs.astype(F32), ((0, 0), (0, 5), (0, 0)))
    groups = filters.shape[1]
    vm = pl.BlockSpec(memory_space=pltpu.VMEM)
    sm = pl.BlockSpec(memory_space=pltpu.SMEM)
    dma = pltpu.SemaphoreType.DMA
    return pl.pallas_call(
        functools.partial(kernel, n_var, n_tp, chunks, width),
        out_shape=jax.ShapeDtypeStruct((2, window_len, full), BF16),
        in_specs=[sm] * 4 + [vm] * 2 + [pl.BlockSpec(memory_space=pl.ANY)] + [vm] * 3,
        out_specs=vm,
        scratch_shapes=[
            pltpu.VMEM((slots, 32, width), BF16),
            pltpu.VMEM(proj.shape, BF16),
            pltpu.VMEM((n_tp, 32, chan), BF16),
            pltpu.VMEM((n_tp, groups, LANES), BF16),
            pltpu.VMEM((12, 40, LANES), F32),
            pltpu.SMEM((2 * n_var,), jnp.int32),
            pltpu.SMEM((variant_position.shape[0],), jnp.int32),
            dma((chunks, n_var)), dma((chunks, n_var)), dma((chunks,)),
            dma((chunks, n_tp)), dma((chunks, n_tp)), dma((chunks,)),
            dma((2, n_tp)), dma((2, n_tp)), dma((2,)), dma((1,)),
        ]
        + [pltpu.VMEM((n_var, ROWS, width), BF16)] * (2 * chunks)
        + [pltpu.VMEM((n_tp, ROWS, width), BF16)] * (2 * chunks),
        compiler_params=pltpu.CompilerParams(
            collective_id=0, has_side_effects=True, vmem_limit_bytes=48 * 1024 * 1024
        ),
        cost_estimate=pl.CostEstimate(flops=6 * 10**9, bytes_accessed=12 * 10**6, transcendentals=0),
    )(window_owner[:, 0], window_slot, variant_position, allele, cache_history, lead, proj, taps, frev, base)


def solution(mesh):
    return jax.shard_map(
        local,
        mesh=mesh,
        in_specs=(
            P(("var", "tp"), None, None, None),
            P("var", None, "tp"),
            P("var", None, None, "tp"),
            P(None, None, "tp"),
            P(None, "tp"),
            P("tp"),
            P(None, None, "tp"),
            P(),
            P(),
            P("var"),
            P("var"),
        ),
        out_specs=P(("var", "tp"), None, None),
        check_vma=False,
    )
```
